32 devices in a mesh: expert: 4 (over y, x), dp: 8 (over z, core).
Axes of the slice: x: 2, y: 2, z: 4, core: 2. Of those that a mesh axis runs over, the one named last changes fastest.
Arguments:
- tokens: bfloat16 [4096, 2048], P(('expert', 'dp')), may hold values from -6 to 6
- cotangent: bfloat16 [4096, 2048], P(('expert', 'dp')), may hold values from -3 to 3
- w_in: bfloat16 [4, 2048, 768], P('expert', 'dp'), may hold values from -0.125 to 0.125
- w_out: bfloat16 [4, 2048, 384], P('expert', 'dp'), may hold values from -0.3125 to 0.3125
- block_rows: int32 [32, 4, 64], P(('expert', 'dp')), may hold values from -1 to 127, as said below
- block_gates: float32 [32, 4, 64], P(('expert', 'dp')), may hold values from 0.1 to 1
- block_count: int32 [32, 2], P(('expert', 'dp')), may hold values from 1 to 2, as said below
Outputs:
- mixed: bfloat16 [4096, 2048], P(('expert', 'dp'))
- token_grad: bfloat16 [4096, 2048], P(('expert', 'dp'))
- gate_grad: float32 [32, 4, 64], P(('expert', 'dp'))
- grad_in: bfloat16 [4, 2048, 768], P('expert', 'dp')
- grad_out: bfloat16 [4, 2048, 384], P('expert', 'dp')
The draws below stay inside these ranges and needn't reach their ends.
Inputs may be any that keep to these rules, and one draw needn't show every extreme that they name: `block_rows`: for each shard and stop, the first block_count blocks list the tokens routed to that stop's expert in increasing order, followed by -1 entries to the end of the last used block; blocks beyond block_count hold arbitrary tokens of the shard. In every shard one stop receives all 128 tokens; each other stop receives a share of them that differs from shard to shard. `block_count`: the number of used blocks of each stop: the stop's routed tokens divided by 64, rounded up.
All inputs are finite; a program needn't handle non-finite values.
Results may differ from the reference program's by a relative error of at most 0.019.
Values may be sent and summed in bfloat16 or wider, within the bound.
A program may use at most 64 MiB of HBM per device.

```python
import jax
import jax.numpy as jnp
from jax import lax

D = 2048
FFW = 384
BLOCK = 64
STOPS = 2
TOK_DEV = 128
MAXB = 2
SLOTS = 4
SHARDS = 32
TOKENS = 4096
EXPERTS = 4
N_DP = 8


def plan_rows(key):
    base_key = jax.random.fold_in(key, 4711)
    key_full, key_other, key_share = jax.random.split(base_key, 3)
    full_stop = jax.random.randint(key_full, (SHARDS,), 0, STOPS).astype(jnp.int32)
    share_cut = jax.random.randint(key_share, (SHARDS,), TOK_DEV // 5, 4 * TOK_DEV // 5 + 1).astype(jnp.int32)
    coin_vals = jax.random.randint(key_other, (SHARDS, TOK_DEV), 0, TOK_DEV).astype(jnp.int32)
    other_pick = coin_vals < share_cut[:, None]
    stop_ids = jnp.arange(STOPS, dtype=jnp.int32)
    is_full = stop_ids[None, :] == full_stop[:, None]
    chosen = is_full[:, :, None] | other_pick[:, None, :]
    filled = jnp.sum(chosen.astype(jnp.int32), axis=-1)
    positions = jnp.arange(TOK_DEV, dtype=jnp.int32)
    sort_keys = jnp.where(chosen, positions, TOK_DEV + positions)
    ordered = jnp.argsort(sort_keys, axis=-1, stable=True).astype(jnp.int32)
    blocks_used = ((filled + BLOCK - 1) // BLOCK).astype(jnp.int32)
    padded = jnp.where(positions < blocks_used[..., None] * BLOCK, -1, ordered)
    entries = jnp.where(positions < filled[..., None], ordered, padded)
    return (entries.reshape(SHARDS, SLOTS, BLOCK).astype(jnp.int32), blocks_used)


def draw_block_rows(key, part):
    return plan_rows(key)[0]


def draw_block_count(key, part):
    return plan_rows(key)[1]


def levels(own_key, extent, cuts, smallest, high):
    def one(dim, blocks):
        steps = jax.random.uniform(jax.random.fold_in(jax.random.fold_in(own_key, 6), dim), (blocks,), jnp.float32, smallest / len(cuts), high / len(cuts))
        return jnp.repeat(jnp.exp(steps), extent[dim] // blocks).reshape((-1,) + (1,) * (len(extent) - dim - 1))

    factor_of = one(*cuts[0])
    for cut in cuts[1:]:
        factor_of = factor_of * one(*cut)
    return factor_of


def bell_draw(key, extent, scale, bound, cuts=(), held_as=jnp.bfloat16):
    values = scale * jax.random.normal(key, extent, jnp.float32)
    if cuts:
        values = values * levels(key, extent, cuts, -0.22, 0.18)
    return jnp.clip(values, -bound, bound).astype(held_as)


def setup_inputs(seed: int = 0) -> dict:
    splits = jax.random.split(jax.random.key(seed), 8)
    return {
        "tokens": bell_draw(splits[0], (TOKENS, D), 1.0, 6.0, ((0, 32),)),
        "cotangent": bell_draw(splits[1], (TOKENS, D), 0.5, 3.0, ((0, 32),)),
        "w_in": bell_draw(splits[2], (EXPERTS, D, 2 * FFW), D ** -0.5, 0.125, ((0, 4), (1, 8))),
        "w_out": bell_draw(splits[3], (EXPERTS, D, FFW), FFW ** -0.5, 0.3125, ((0, 4), (1, 8))),
        "block_rows": draw_block_rows(jax.random.fold_in(splits[7], 71), 0),
        "block_gates": jnp.clip(0.1 + 0.9 * jax.random.uniform(splits[5], (SHARDS, SLOTS, BLOCK), jnp.float32) ** levels(splits[5], (SHARDS, SLOTS, BLOCK), ((0, 32),), -0.2, 0.2), 0.1, 1.0),
        "block_count": draw_block_count(jax.random.fold_in(splits[7], 71), 0),
    }


def silu_pair(preact):
    sigmoid_val = jax.nn.sigmoid(preact)
    return preact * sigmoid_val, sigmoid_val * (1.0 + preact * (1.0 - sigmoid_val))


def contract_rows(left_mat, right_mat):
    return lax.dot_general(left_mat, right_mat, (((0,), (0,)), ((), ())), preferred_element_type=jnp.float32)


def contract_cols(left_mat, right_mat):
    return lax.dot_general(left_mat, right_mat, (((1,), (1,)), ((), ())), preferred_element_type=jnp.float32)


def expert_pass(inputs, gated_cot, slab_in, slab_out):
    hidden_width = slab_out.shape[1]
    preact = jnp.dot(inputs, slab_in, preferred_element_type=jnp.float32)
    gate_pre = preact[:, :hidden_width]
    up_pre = preact[:, hidden_width:]
    activated, derivative = silu_pair(gate_pre)
    hidden = (activated * up_pre).astype(jnp.bfloat16)
    output = contract_cols(hidden, slab_out)
    act_grad = jnp.dot(gated_cot, slab_out, preferred_element_type=jnp.float32)
    hid_grad = jnp.concatenate([act_grad * up_pre * derivative, act_grad * activated], axis=1).astype(jnp.bfloat16)
    input_grad = contract_cols(hid_grad, slab_in)
    return output, input_grad, hidden, hid_grad


def slot_masks(entries, gate_vals, block_total):
    positions = jnp.arange(entries.shape[0], dtype=jnp.int32)
    live_mask = ((positions // BLOCK < block_total) & (entries >= 0)).astype(jnp.float32)
    token_ids = jnp.where(entries >= 0, entries, 0).astype(jnp.int32)
    return live_mask, token_ids, gate_vals * live_mask


def reference(tokens, cotangent, w_in, w_out, block_rows, block_gates, block_count):
    slot_span = MAXB * BLOCK
    token_blocks = tokens.reshape(SHARDS, TOK_DEV, D)
    cot_blocks = cotangent.reshape(SHARDS, TOK_DEV, D)
    row_blocks = block_rows.reshape(SHARDS, STOPS, slot_span)
    gate_blocks = block_gates.reshape(SHARDS, STOPS, slot_span)

    def one_shard(running, packed):
        sum_in, sum_out = running
        shard_id, inputs_all, cot_block, row_table, gate_table, block_total = packed
        cycle_pos = shard_id // N_DP
        mixed_sum = jnp.zeros((TOK_DEV, D), jnp.float32)
        token_sum = jnp.zeros((TOK_DEV, D), jnp.float32)
        gate_list = []
        for station in range(STOPS):
            expert = ((cycle_pos - station) % EXPERTS).astype(jnp.int32)
            live_mask, token_ids, weight = slot_masks(row_table[station], gate_table[station], block_total[station])
            inputs = inputs_all[token_ids]
            cot_rows = cot_block[token_ids]
            gated_cot = (weight[:, None] * cot_rows.astype(jnp.float32)).astype(jnp.bfloat16)
            output, input_grad, hidden, hid_grad = expert_pass(inputs, gated_cot, w_in[expert], w_out[expert])
            mixed_sum = mixed_sum.at[token_ids].add(weight[:, None] * output)
            token_sum = token_sum.at[token_ids].add(input_grad)
            gate_list.append(live_mask * jnp.sum(output * cot_rows.astype(jnp.float32), axis=1))
            term_in = contract_rows(inputs, hid_grad).astype(jnp.bfloat16)
            term_out = contract_rows(gated_cot, hidden).astype(jnp.bfloat16)
            term_in, term_out = lax.optimization_barrier((term_in, term_out))
            sum_in = sum_in.at[expert].add(term_in.astype(jnp.float32))
            sum_out = sum_out.at[expert].add(term_out.astype(jnp.float32))
        outputs = (mixed_sum.astype(jnp.bfloat16), token_sum.astype(jnp.bfloat16), jnp.stack(gate_list))
        return (sum_in, sum_out), outputs

    initial = (jnp.zeros((EXPERTS, D, 2 * FFW), jnp.float32), jnp.zeros((EXPERTS, D, FFW), jnp.float32))
    shard_ids = jnp.arange(SHARDS, dtype=jnp.int32)
    totals, results = lax.scan(one_shard, initial, (shard_ids, token_blocks, cot_blocks, row_blocks, gate_blocks, block_count))
    mixed = results[0].reshape(TOKENS, D)
    token_grad = results[1].reshape(TOKENS, D)
    gate_grad = results[2].reshape(SHARDS, SLOTS, BLOCK)
    return mixed, token_grad, gate_grad, totals[0].astype(jnp.bfloat16), totals[1].astype(jnp.bfloat16)
```

```python
import jax
import jax.numpy as jnp
from jax import lax
from jax.sharding import PartitionSpec as P


def shifted(block, axis, distance):
    devices = range(lax.axis_size(axis))
    route = [((i - distance) % len(devices), i) for i in devices]
    return lax.ppermute(block, axis, route)


def contract_rows(left_mat, right_mat):
    return lax.dot_general(
        left_mat, right_mat, (((0,), (0,)), ((), ())), preferred_element_type=jnp.float32
    )


def contract_cols(left_mat, right_mat):
    return lax.dot_general(
        left_mat, right_mat, (((1,), (1,)), ((), ())), preferred_element_type=jnp.float32
    )


def body(tokens, cotangent, w_in, w_out, block_rows, block_gates, block_count):
    stops = block_count.shape[1]
    block_size = block_rows.shape[2]
    span = block_rows.shape[1] // stops * block_size
    rows = tokens.shape[0]
    ffw = w_out.shape[2]
    bf16, f32 = jnp.bfloat16, jnp.float32
    entries = block_rows.reshape(stops, span)
    gates = block_gates.reshape(stops, span)
    counts = block_count[0]
    positions = jnp.arange(span, dtype=jnp.int32)
    live = (positions[None, :] // block_size < counts[:, None]) & (entries >= 0)
    pick = (
        live[:, :, None] & (entries[:, :, None] == jnp.arange(rows, dtype=jnp.int32))
    ).astype(f32)
    gate_of = jnp.sum(pick * gates[:, :, None], axis=1)

    slab_in = lax.all_gather(w_in[0], "dp", axis=0, tiled=True)
    slab_out = lax.all_gather(w_out[0], "dp", axis=0, tiled=True)
    xs, cs, gs = [tokens], [cotangent], [gate_of[0]]
    for k in range(1, stops):
        x, c, g = shifted((tokens, cotangent, gate_of[k]), "expert", -k)
        xs.append(x)
        cs.append(c)
        gs.append(g)
    x, c, g = jnp.concatenate(xs), jnp.concatenate(cs), jnp.concatenate(gs)[:, None]
    pre = jnp.dot(x, slab_in, preferred_element_type=f32)
    h, u = pre[:, :ffw], pre[:, ffw:]
    dc = jnp.dot(c, slab_out, preferred_element_type=f32)
    sig = jax.nn.sigmoid(h)
    act = h * sig
    a = act * u
    gate_tok = jnp.sum(a * dc, axis=1)
    da = g * dc
    ag = (g * a).astype(bf16)
    hg = jnp.concatenate([da * u * (sig * (1.0 + h * (1.0 - sig))), da * act], axis=1).astype(bf16)
    o = contract_cols(ag, slab_out)
    tg = contract_cols(hg, slab_in)
    mixed, token_grad, gate_parts = o[:rows], tg[:rows], [gate_tok[:rows]]
    for k in range(1, stops):
        cut = slice(k * rows, (k + 1) * rows)
        po, pt, pg = shifted((o[cut].astype(bf16), tg[cut].astype(bf16), gate_tok[cut]), "expert", k)
        mixed = mixed + po.astype(f32)
        token_grad = token_grad + pt.astype(f32)
        gate_parts.append(pg)
    term = jnp.concatenate([contract_rows(x, hg), contract_rows(c, ag)], axis=1).astype(bf16)
    total = lax.psum_scatter(term, "dp", scatter_dimension=0, tiled=True)
    gate_grad = jnp.sum(pick * jnp.stack(gate_parts)[:, None, :], axis=2).reshape(block_rows.shape)
    return (
        mixed.astype(bf16),
        token_grad.astype(bf16),
        gate_grad,
        total[:, : 2 * ffw][None],
        total[:, 2 * ffw :][None],
    )


def solution(mesh):
    in_specs = (
        P(("expert", "dp"), None),
        P(("expert", "dp"), None),
        P("expert", "dp", None),
        P("expert", "dp", None),
        P(("expert", "dp"), None, None),
        P(("expert", "dp"), None, None),
        P(("expert", "dp"), None),
    )
    out_specs = (
        P(("expert", "dp"), None),
        P(("expert", "dp"), None),
        P(("expert", "dp"), None, None),
        P("expert", "dp", None),
        P("expert", "dp", None),
    )
    return jax.shard_map(body, mesh=mesh, in_specs=in_specs, out_specs=out_specs, check_vma=False)
```

```python
import functools

import jax
import jax.numpy as jnp
from jax import lax
from jax.experimental import pallas as pl
from jax.experimental.pallas import tpu as pltpu
from jax.sharding import PartitionSpec as P

BF16, F32 = jnp.bfloat16, jnp.float32
MESH = pl.DeviceIdType.MESH
LANES = 128


def dot_nn(left, right):
    return jnp.dot(left, right, preferred_element_type=F32)


def dot_nt(left, right):
    return lax.dot_general(left, right, (((1,), (1,)), ((), ())), preferred_element_type=F32)


def kernel(
    dims,
    tok_ref,
    cot_ref,
    win_ref,
    wout_ref,
    meta_ref,
    mixed_ref,
    tgrad_ref,
    gate_ref,
    gin_ref,
    gout_ref,
    xa,
    ca,
    ma,
    w,
    xt,
    ct,
    xts,
    cts,
    hid,
    part,
    rbr,
    rbl,
    o0,
    t0,
    ob,
    tb,
    gb,
    ro,
    rt,
    rg,
    acc,
    s_agr,
    r_agr,
    s_agl,
    r_agl,
    s_sib,
    r_sib,
    s_xt,
    r_xt,
    s_hid,
    r_hid,
    s_rsr,
    r_rsr,
    s_rsl,
    r_rsl,
    s_tok,
    r_tok,
    s_ret,
    r_ret,
    s_rg,
    r_rg,
):
    n_exp, n_dp, stops = dims
    n = n_dp // 2
    rows, width = tok_ref.shape
    sr, ffw = wout_ref.shape
    qw = LANES
    nq = ffw // qw
    span = meta_ref.shape[2]
    td = next(t for t in (512, 256, 128) if width % t == 0)
    tiles = width // td

    e = lax.axis_index("expert")
    d = lax.axis_index("dp")
    z = d // 2
    c = d % 2
    has_l = z > 0
    has_r = z < n - 1
    right = {"expert": e, "dp": d + 2}
    left = {"expert": e, "dp": d - 2}
    sib = {"expert": e, "dp": 2 * z + (1 - c)}

    def cycle(k):
        return {"expert": (e + k) % n_exp, "dp": d}

    def remote(src, dst, ss, rs, dev):
        return pltpu.make_async_remote_copy(
            src_ref=src, dst_ref=dst, send_sem=ss, recv_sem=rs, device_id=dev, device_id_type=MESH
        )

    offsets = sorted({k % n_exp for k in range(1, stops)} | {-k % n_exp for k in range(1, stops)})
    barrier = pltpu.get_barrier_semaphore()
    pl.semaphore_signal(barrier, inc=1, device_id=sib, device_id_type=MESH)
    for k in offsets:
        pl.semaphore_signal(barrier, inc=1, device_id=cycle(k), device_id_type=MESH)

    @pl.when(has_l)
    def _():
        pl.semaphore_signal(barrier, inc=1, device_id=left, device_id_type=MESH)

    @pl.when(has_r)
    def _():
        pl.semaphore_signal(barrier, inc=1, device_id=right, device_id_type=MESH)

    own = pl.ds(pl.multiple_of(d * sr, 16), sr)
    for q in range(nq):
        w[q, own, 0:qw] = win_ref[:, q * qw : (q + 1) * qw]
        w[q, own, qw : 2 * qw] = win_ref[:, ffw + q * qw : ffw + (q + 1) * qw]
        w[q, own, 2 * qw : 3 * qw] = wout_ref[:, q * qw : (q + 1) * qw]
    neighbours = jnp.where(has_l, 1, 0) + jnp.where(has_r, 1, 0)
    pl.semaphore_wait(barrier, 1 + len(offsets) + neighbours)

    def shard(q, chip, core):
        return w.at[q, pl.ds(pl.multiple_of((2 * chip + core) * sr, 16), sr)]

    def ag_right(q, i):
        ref = shard(q, z - i, c)
        return remote(ref, ref, s_agr.at[q, i], r_agr.at[q, i], right)

    def ag_left(q, i):
        ref = shard(q, z + i, c)
        return remote(ref, ref, s_agl.at[q, i], r_agl.at[q, i], left)

    def from_left(q, i):
        ref = shard(q, z - 1 - i, c)
        return remote(ref, ref, s_agr.at[q, i], r_agr.at[q, i], left)

    def from_right(q, i):
        ref = shard(q, z + 1 + i, c)
        return remote(ref, ref, s_agl.at[q, i], r_agl.at[q, i], right)

    def ag_sib(q, chip, index, core):
        ref = shard(q, chip, core)
        return remote(ref, ref, s_sib.at[q, index], r_sib.at[q, index], sib)

    def tok_copies(k):
        cut = pl.ds(k * rows, rows)
        return [
            remote(tok_ref, xa.at[cut], s_tok.at[k, 0], r_tok.at[k, 0], cycle(-k)),
            remote(cot_ref, ca.at[cut], s_tok.at[k, 1], r_tok.at[k, 1], cycle(-k)),
            remote(meta_ref.at[k], ma.at[k], s_tok.at[k, 2], r_tok.at[k, 2], cycle(-k)),
        ]

    def xt_copies():
        return [
            remote(xt.at[:, 1 - c], xts, s_xt.at[0], r_xt.at[0], sib),
            remote(ct.at[:, 1 - c], cts, s_xt.at[1], r_xt.at[1], sib),
        ]

    def hid_copy(q, core):
        ref = hid.at[q, core]
        return remote(ref, ref, s_hid.at[q], r_hid.at[q], sib)

    def rs_right(q, t):
        return remote(part.at[q, t], rbr.at[q, t], s_rsr.at[q, t], r_rsr.at[q, t], right)

    def rs_left(q, t):
        return remote(part.at[q, t], rbl.at[q, t], s_rsl.at[q, t], r_rsl.at[q, t], left)

    def ret_copies(k, j):
        cut = (k, slice(None), pl.ds(j * td, td))
        return [
            remote(ob.at[cut], ro.at[cut], s_ret.at[k, j, 0], r_ret.at[k, j, 0], cycle(k)),
            remote(tb.at[cut], rt.at[cut], s_ret.at[k, j, 1], r_ret.at[k, j, 1], cycle(k)),
        ]

    def gate_copy(k):
        return remote(gb.at[k], rg.at[k], s_rg.at[k], r_rg.at[k], cycle(k))

    def ag_own(q):
        @pl.when(has_r)
        def _():
            ag_right(q, 0).start()

        @pl.when(has_l)
        def _():
            ag_left(q, 0).start()

        ag_sib(q, z, 0, c).start()

    def ag_step(q, i):
        @pl.when(z - 1 - i >= 0)
        def _():
            from_left(q, i).wait_recv()

            @pl.when(has_r)
            def _():
                ag_right(q, i + 1).start()

            ag_sib(q, z - 1 - i, 1 + i, c).start()

        @pl.when(z + 1 + i <= n - 1)
        def _():
            from_right(q, i).wait_recv()

            @pl.when(has_l)
            def _():
                ag_left(q, i + 1).start()

            ag_sib(q, z + 1 + i, n + i, c).start()

    def ag_join(q):
        ag_sib(q, z, 0, 1 - c).wait_recv()
        for i in range(n - 1):

            @pl.when(z - 1 - i >= 0)
            def _():
                ag_sib(q, z - 1 - i, 1 + i, 1 - c).wait_recv()

            @pl.when(z + 1 + i <= n - 1)
            def _():
                ag_sib(q, z + 1 + i, n + i, 1 - c).wait_recv()

    def rs_step(q, j):
        t = n - 1 - j

        @pl.when(t > z)
        def _():
            @pl.when(has_l)
            def _():
                rs_right(q, t).wait_recv()
                part[q, t] = (part[q, t].astype(F32) + rbr[q, t].astype(F32)).astype(BF16)

            rs_right(q, t).start()

        @pl.when(j < z)
        def _():
            @pl.when(has_r)
            def _():
                rs_left(q, j).wait_recv()
                part[q, j] = (part[q, j].astype(F32) + rbl[q, j].astype(F32)).astype(BF16)

            rs_left(q, j).start()

    def rs_finish(q):
        total = part[q, z].astype(F32)
        acc[...] = total

        @pl.when(has_l)
        def _():
            rs_right(q, z).wait_recv()
            acc[...] += rbr[q, z].astype(F32)

        @pl.when(has_r)
        def _():
            rs_left(q, z).wait_recv()
            acc[...] += rbl[q, z].astype(F32)

        done = acc[...].astype(BF16)
        gin_ref[:, q * qw : (q + 1) * qw] = done[:, 0:qw]
        gin_ref[:, ffw + q * qw : ffw + (q + 1) * qw] = done[:, qw : 2 * qw]
        gout_ref[:, q * qw : (q + 1) * qw] = done[:, 2 * qw : 3 * qw]

    def turn(k):
        cut = slice(k * rows, (k + 1) * rows)
        xt[:, :, :, cut] = xa[cut, :].T.reshape(n, 2, sr, rows)
        ct[:, :, :, cut] = ca[cut, :].T.reshape(n, 2, sr, rows)

    def pick_of(k):
        return jnp.where(
            lax.broadcasted_iota(jnp.int32, (rows, span), 0).astype(F32) == ma[k, 0:1, :], 1.0, 0.0
        )

    def forward(q, gates):
        pre = dot_nn(xa[...], w[q, :, 0 : 2 * qw])
        dc = dot_nn(ca[...], w[q, :, 2 * qw : 3 * qw])
        h, u = pre[:, :qw], pre[:, qw:]
        sig = jax.nn.sigmoid(h)
        act = h * sig
        a = act * u
        da = gates * dc
        hid[q, c, :, 0:qw] = (da * u * (sig * (1.0 + h * (1.0 - sig)))).astype(BF16)
        hid[q, c, :, qw : 2 * qw] = (da * act).astype(BF16)
        hid[q, c, :, 2 * qw : 3 * qw] = (gates * a).astype(BF16)
        hid_copy(q, c).start()
        return jnp.sum(a * dc, axis=1, keepdims=True)

    def terms(q):
        hid_copy(q, 1 - c).wait_recv()
        mine, theirs = hid[q, c], hid[q, 1 - c]

        def one(t, carry):
            part[q, t, :, 0 : 2 * qw] = (
                dot_nn(xt[t, c], mine[:, 0 : 2 * qw]) + dot_nn(xts[t], theirs[:, 0 : 2 * qw])
            ).astype(BF16)
            part[q, t, :, 2 * qw : 3 * qw] = (
                dot_nn(ct[t, c], mine[:, 2 * qw :]) + dot_nn(cts[t], theirs[:, 2 * qw :])
            ).astype(BF16)
            return carry

        lax.fori_loop(0, n, one, 0)

    for k in range(1, stops):
        for copy in tok_copies(k):
            copy.start()
    ag_own(0)
    xa[0:rows, :] = tok_ref[...]
    ca[0:rows, :] = cot_ref[...]
    ma[0] = meta_ref[0]
    turn(0)
    for i in range(n - 1):
        ag_step(0, i)
    if nq > 1:
        ag_own(1)
        for i in range(n - 1):
            ag_step(1, i)
    for k in range(1, stops):
        for copy in tok_copies(k):
            copy.wait_recv()
    if nq > 2:
        ag_own(2)
    for k in range(1, stops):
        turn(k)
    for copy in xt_copies():
        copy.start()
    gates = jnp.concatenate(
        [jnp.sum(pick_of(k) * ma[k, 1:2, :], axis=1, keepdims=True) for k in range(stops)]
    )
    gate_sum = jnp.zeros((stops * rows, 1), F32)
    for q in range(nq):
        if q >= 2:
            for i in range(n - 1):
                ag_step(q, i)
                rs_step(q - 2, i)
            if q + 1 < nq:
                ag_own(q + 1)
        ag_join(q)
        gate_sum = gate_sum + forward(q, gates)
        if q == 0:
            for copy in xt_copies():
                copy.wait_recv()
        if q < nq - 1:
            terms(q)

    for k in range(stops):
        gt = gate_sum[k * rows : (k + 1) * rows]
        row = jnp.sum(pick_of(k) * gt, axis=0, keepdims=True)
        if k == 0:
            gate_ref[0] = jnp.broadcast_to(row, (8, span))
        else:
            gb[k] = jnp.broadcast_to(row, (8, span))
            gate_copy(k).start()
    for j in range(tiles):
        cut = slice(j * td, (j + 1) * td)
        out = sum(dot_nt(hid[q, c, :, 2 * qw :], w[q, cut, 2 * qw :]) for q in range(nq))
        tok = sum(dot_nt(hid[q, c, :, : 2 * qw], w[q, cut, : 2 * qw]) for q in range(nq))
        o0[:, cut] = out[:rows]
        t0[:, cut] = tok[:rows]
        for k in range(1, stops):
            ob[k, :, cut] = out[k * rows : (k + 1) * rows].astype(BF16)
            tb[k, :, cut] = tok[k * rows : (k + 1) * rows].astype(BF16)
            for copy in ret_copies(k, j):
                copy.start()
    terms(nq - 1)
    for q in range(max(nq - 2, 0), nq):
        for i in range(n - 1):
            rs_step(q, i)

    for k in range(1, stops):
        gate_copy(k).wait_recv()
        gate_ref[k] = rg[k]
        for j in range(tiles):
            for copy in ret_copies(k, j):
                copy.wait_recv()
    mixed, tgrad = o0[...], t0[...]
    for k in range(1, stops):
        mixed = mixed + ro[k].astype(F32)
        tgrad = tgrad + rt[k].astype(F32)
    mixed_ref[...] = mixed.astype(BF16)
    tgrad_ref[...] = tgrad.astype(BF16)
    for q in range(nq):
        rs_finish(q)

    for k in range(1, stops):
        for copy in tok_copies(k):
            copy.wait_send()
        gate_copy(k).wait_send()
        for j in range(tiles):
            for copy in ret_copies(k, j):
                copy.wait_send()
    for copy in xt_copies():
        copy.wait_send()
    for q in range(nq):
        hid_copy(q, c).wait_send()
        ag_sib(q, z, 0, c).wait_send()
        for i in range(n - 1):

            @pl.when((z - i >= 0) & has_r)
            def _():
                ag_right(q, i).wait_send()

            @pl.when((z + i <= n - 1) & has_l)
            def _():
                ag_left(q, i).wait_send()

            @pl.when(z - 1 - i >= 0)
            def _():
                ag_sib(q, z - 1 - i, 1 + i, c).wait_send()

            @pl.when(z + 1 + i <= n - 1)
            def _():
                ag_sib(q, z + 1 + i, n + i, c).wait_send()

            @pl.when(n - 1 - i > z)
            def _():
                rs_right(q, n - 1 - i).wait_send()

            @pl.when(i < z)
            def _():
                rs_left(q, i).wait_send()


def body(n_exp, n_dp, tokens, cotangent, w_in, w_out, block_rows, block_gates, block_count):
    stops = block_count.shape[1]
    block = block_rows.shape[2]
    span = block_rows.shape[1] // stops * block
    rows, width = tokens.shape
    sr, ffw = w_out.shape[1:]
    n, nq, total = n_dp // 2, ffw // LANES, stops * rows
    tiles = width // next(t for t in (512, 256, 128) if width % t == 0)
    entries = block_rows.reshape(stops, span)
    gates = block_gates.reshape(stops, span)
    positions = jnp.arange(span, dtype=jnp.int32)
    live = positions[None, :] // block < block_count[0][:, None]
    ids = jnp.where(live, entries, -1).astype(F32)
    pick = jnp.arange(8)[None, :, None]
    meta = jnp.where(pick == 0, ids[:, None, :], gates[:, None, :])

    dma = pltpu.SemaphoreType.DMA
    vmem = pltpu.VMEM
    mixed, tgrad, gate, gin, gout = pl.pallas_call(
        functools.partial(kernel, (n_exp, n_dp, stops)),
        out_shape=(
            jax.ShapeDtypeStruct((rows, width), BF16),
            jax.ShapeDtypeStruct((rows, width), BF16),
            jax.ShapeDtypeStruct((stops, 8, span), F32),
            jax.ShapeDtypeStruct((sr, 2 * ffw), BF16),
            jax.ShapeDtypeStruct((sr, ffw), BF16),
        ),
        in_specs=[pl.BlockSpec(memory_space=vmem)] * 5,
        out_specs=(pl.BlockSpec(memory_space=vmem),) * 5,
        scratch_shapes=[
            vmem((total, width), BF16),
            vmem((total, width), BF16),
            vmem((stops, 8, span), F32),
            vmem((nq, n_dp * sr, 3 * LANES), BF16),
            vmem((n, 2, sr, total), BF16),
            vmem((n, 2, sr, total), BF16),
            vmem((n, sr, total), BF16),
            vmem((n, sr, total), BF16),
            vmem((nq, 2, total, 3 * LANES), BF16),
            vmem((nq, n, sr, 3 * LANES), BF16),
            vmem((nq, n, sr, 3 * LANES), BF16),
            vmem((nq, n, sr, 3 * LANES), BF16),
            vmem((rows, width), F32),
            vmem((rows, width), F32),
            vmem((stops, rows, width), BF16),
            vmem((stops, rows, width), BF16),
            vmem((stops, 8, span), F32),
            vmem((stops, rows, width), BF16),
            vmem((stops, rows, width), BF16),
            vmem((stops, 8, span), F32),
            vmem((sr, 3 * LANES), F32),
            dma((nq, n)),
            dma((nq, n)),
            dma((nq, n)),
            dma((nq, n)),
            dma((nq, 2 * n)),
            dma((nq, 2 * n)),
            dma((2,)),
            dma((2,)),
            dma((nq,)),
            dma((nq,)),
            dma((nq, n)),
            dma((nq, n)),
            dma((nq, n)),
            dma((nq, n)),
            dma((stops, 3)),
            dma((stops, 3)),
            dma((stops, tiles, 2)),
            dma((stops, tiles, 2)),
            dma((stops,)),
            dma((stops,)),
        ],
        compiler_params=pltpu.CompilerParams(
            collective_id=0, has_side_effects=True, vmem_limit_bytes=56 * 1024 * 1024
        ),
        cost_estimate=pl.CostEstimate(
            flops=6 * total * width * 3 * ffw, bytes_accessed=8 * rows * width, transcendentals=0
        ),
    )(tokens, cotangent, w_in[0], w_out[0], meta)
    return mixed, tgrad, gate[:, 0].reshape(block_rows.shape), gin[None], gout[None]


def solution(mesh):
    in_specs = (
        P(("expert", "dp"), None),
        P(("expert", "dp"), None),
        P("expert", "dp", None),
        P("expert", "dp", None),
        P(("expert", "dp"), None, None),
        P(("expert", "dp"), None, None),
        P(("expert", "dp"), None),
    )
    out_specs = (
        P(("expert", "dp"), None),
        P(("expert", "dp"), None),
        P(("expert", "dp"), None, None),
        P("expert", "dp", None),
        P("expert", "dp", None),
    )
    run = functools.partial(body, mesh.shape["expert"], mesh.shape["dp"])
    return jax.shard_map(run, mesh=mesh, in_specs=in_specs, out_specs=out_specs, check_vma=False)
```

```python
import functools

import jax
import jax.numpy as jnp
from jax import lax
from jax.experimental import pallas as pl
from jax.experimental.pallas import tpu as pltpu
from jax.sharding import PartitionSpec as P

BF16, F32 = jnp.bfloat16, jnp.float32
MESH = pl.DeviceIdType.MESH
LANES = 128


def dot_nn(left, right):
    return jnp.dot(left, right, preferred_element_type=F32)


def dot_nt(left, right):
    return lax.dot_general(left, right, (((1,), (1,)), ((), ())), preferred_element_type=F32)


def kernel(
    dims,
    tok_ref,
    cot_ref,
    win_ref,
    wout_ref,
    meta_ref,
    mixed_ref,
    tgrad_ref,
    gate_ref,
    gin_ref,
    gout_ref,
    xa,
    ca,
    ma,
    w,
    xt,
    ct,
    xts,
    cts,
    hid,
    part,
    rbr,
    rbl,
    o0,
    t0,
    ob,
    tb,
    gb,
    ro,
    rt,
    rg,
    acc,
    s_agr,
    r_agr,
    s_agl,
    r_agl,
    s_sib,
    r_sib,
    s_xt,
    r_xt,
    s_hid,
    r_hid,
    s_rsr,
    r_rsr,
    s_rsl,
    r_rsl,
    s_tok,
    r_tok,
    s_ret,
    r_ret,
    s_rg,
    r_rg,
):
    n_exp, n_dp, stops = dims
    n = n_dp // 2
    rows, width = tok_ref.shape
    sr, ffw = wout_ref.shape
    qw = LANES
    nq = ffw // qw
    span = meta_ref.shape[2]
    td = next(t for t in (512, 256, 128) if width % t == 0)
    tiles = width // td

    e = lax.axis_index("expert")
    d = lax.axis_index("dp")
    z = d // 2
    c = d % 2
    has_l = z > 0
    has_r = z < n - 1
    right = {"expert": e, "dp": d + 2}
    left = {"expert": e, "dp": d - 2}
    sib = {"expert": e, "dp": 2 * z + (1 - c)}

    def cycle(k):
        return {"expert": (e + k) % n_exp, "dp": d}

    def remote(src, dst, ss, rs, dev):
        return pltpu.make_async_remote_copy(
            src_ref=src, dst_ref=dst, send_sem=ss, recv_sem=rs, device_id=dev, device_id_type=MESH
        )

    offsets = sorted({k % n_exp for k in range(1, stops)} | {-k % n_exp for k in range(1, stops)})
    barrier = pltpu.get_barrier_semaphore()
    pl.semaphore_signal(barrier, inc=1, device_id=sib, device_id_type=MESH)
    for k in offsets:
        pl.semaphore_signal(barrier, inc=1, device_id=cycle(k), device_id_type=MESH)

    @pl.when(has_l)
    def _():
        pl.semaphore_signal(barrier, inc=1, device_id=left, device_id_type=MESH)

    @pl.when(has_r)
    def _():
        pl.semaphore_signal(barrier, inc=1, device_id=right, device_id_type=MESH)

    own = pl.ds(pl.multiple_of(d * sr, 16), sr)
    for q in range(nq):
        w[q, own, 0:qw] = win_ref[:, q * qw : (q + 1) * qw]
        w[q, own, qw : 2 * qw] = win_ref[:, ffw + q * qw : ffw + (q + 1) * qw]
        w[q, own, 2 * qw : 3 * qw] = wout_ref[:, q * qw : (q + 1) * qw]
    neighbours = jnp.where(has_l, 1, 0) + jnp.where(has_r, 1, 0)
    pl.semaphore_wait(barrier, 1 + len(offsets) + neighbours)

    def shard(q, chip, core):
        return w.at[q, pl.ds(pl.multiple_of((2 * chip + core) * sr, 16), sr)]

    def ag_right(q, i):
        ref = shard(q, z - i, c)
        return remote(ref, ref, s_agr.at[q, i], r_agr.at[q, i], right)

    def ag_left(q, i):
        ref = shard(q, z + i, c)
        return remote(ref, ref, s_agl.at[q, i], r_agl.at[q, i], left)

    def from_left(q, i):
        ref = shard(q, z - 1 - i, c)
        return remote(ref, ref, s_agr.at[q, i], r_agr.at[q, i], left)

    def from_right(q, i):
        ref = shard(q, z + 1 + i, c)
        return remote(ref, ref, s_agl.at[q, i], r_agl.at[q, i], right)

    def ag_sib(q, chip, index, core):
        ref = shard(q, chip, core)
        return remote(ref, ref, s_sib.at[q, index], r_sib.at[q, index], sib)

    def tok_copies(k):
        cut = pl.ds(k * rows, rows)
        return [
            remote(tok_ref, xa.at[cut], s_tok.at[k, 0], r_tok.at[k, 0], cycle(-k)),
            remote(cot_ref, ca.at[cut], s_tok.at[k, 1], r_tok.at[k, 1], cycle(-k)),
            remote(meta_ref.at[k], ma.at[k], s_tok.at[k, 2], r_tok.at[k, 2], cycle(-k)),
        ]

    def xt_copies():
        return [
            remote(xt.at[:, 1 - c], xts, s_xt.at[0], r_xt.at[0], sib),
            remote(ct.at[:, 1 - c], cts, s_xt.at[1], r_xt.at[1], sib),
        ]

    def hid_copy(q, core):
        ref = hid.at[q, core]
        return remote(ref, ref, s_hid.at[q], r_hid.at[q], sib)

    def rs_right(q, t):
        return remote(part.at[q, t], rbr.at[q, t], s_rsr.at[q, t], r_rsr.at[q, t], right)

    def rs_left(q, t):
        return remote(part.at[q, t], rbl.at[q, t], s_rsl.at[q, t], r_rsl.at[q, t], left)

    def ret_copies(k, j):
        cut = (k, slice(None), pl.ds(j * td, td))
        return [
            remote(ob.at[cut], ro.at[cut], s_ret.at[k, j, 0], r_ret.at[k, j, 0], cycle(k)),
            remote(tb.at[cut], rt.at[cut], s_ret.at[k, j, 1], r_ret.at[k, j, 1], cycle(k)),
        ]

    def gate_copy(k):
        return remote(gb.at[k], rg.at[k], s_rg.at[k], r_rg.at[k], cycle(k))

    def ag_own(q):
        @pl.when(has_r)
        def _():
            ag_right(q, 0).start()

        @pl.when(has_l)
        def _():
            ag_left(q, 0).start()

        ag_sib(q, z, 0, c).start()

    def ag_step(q, i):
        @pl.when(z - 1 - i >= 0)
        def _():
            from_left(q, i).wait_recv()

            @pl.when(has_r)
            def _():
                ag_right(q, i + 1).start()

            ag_sib(q, z - 1 - i, 1 + i, c).start()

        @pl.when(z + 1 + i <= n - 1)
        def _():
            from_right(q, i).wait_recv()

            @pl.when(has_l)
            def _():
                ag_left(q, i + 1).start()

            ag_sib(q, z + 1 + i, n + i, c).start()

    def ag_join(q):
        ag_sib(q, z, 0, 1 - c).wait_recv()
        for i in range(n - 1):

            @pl.when(z - 1 - i >= 0)
            def _():
                ag_sib(q, z - 1 - i, 1 + i, 1 - c).wait_recv()

            @pl.when(z + 1 + i <= n - 1)
            def _():
                ag_sib(q, z + 1 + i, n + i, 1 - c).wait_recv()

    def rs_step(q, j):
        t = n - 1 - j

        @pl.when(t > z)
        def _():
            @pl.when(has_l)
            def _():
                rs_right(q, t).wait_recv()
                part[q, t] = (part[q, t].astype(F32) + rbr[q, t].astype(F32)).astype(BF16)

            rs_right(q, t).start()

        @pl.when(j < z)
        def _():
            @pl.when(has_r)
            def _():
                rs_left(q, j).wait_recv()
                part[q, j] = (part[q, j].astype(F32) + rbl[q, j].astype(F32)).astype(BF16)

            rs_left(q, j).start()

    def rs_finish(q):
        total = part[q, z].astype(F32)
        acc[...] = total

        @pl.when(has_l)
        def _():
            rs_right(q, z).wait_recv()
            acc[...] += rbr[q, z].astype(F32)

        @pl.when(has_r)
        def _():
            rs_left(q, z).wait_recv()
            acc[...] += rbl[q, z].astype(F32)

        done = acc[...].astype(BF16)
        gin_ref[:, q * qw : (q + 1) * qw] = done[:, 0:qw]
        gin_ref[:, ffw + q * qw : ffw + (q + 1) * qw] = done[:, qw : 2 * qw]
        gout_ref[:, q * qw : (q + 1) * qw] = done[:, 2 * qw : 3 * qw]

    def turn(k):
        cut = slice(k * rows, (k + 1) * rows)
        xt[:, :, :, cut] = xa[cut, :].T.reshape(n, 2, sr, rows)
        ct[:, :, :, cut] = ca[cut, :].T.reshape(n, 2, sr, rows)

    def pick_of(k):
        return jnp.where(
            lax.broadcasted_iota(jnp.int32, (rows, span), 0).astype(F32) == ma[k, 0:1, :], 1.0, 0.0
        )

    def forward(q, gates):
        pre = dot_nn(xa[...], w[q, :, 0 : 2 * qw])
        dc = dot_nn(ca[...], w[q, :, 2 * qw : 3 * qw])
        h, u = pre[:, :qw], pre[:, qw:]
        sig = jax.nn.sigmoid(h)
        act = h * sig
        a = act * u
        da = gates * dc
        hid[q, c, :, 0:qw] = (da * u * (sig * (1.0 + h * (1.0 - sig)))).astype(BF16)
        hid[q, c, :, qw : 2 * qw] = (da * act).astype(BF16)
        hid[q, c, :, 2 * qw : 3 * qw] = (gates * a).astype(BF16)
        hid_copy(q, c).start()
        return jnp.sum(a * dc, axis=1, keepdims=True)

    def terms(q):
        hid_copy(q, 1 - c).wait_recv()
        mine, theirs = hid[q, c], hid[q, 1 - c]

        def one(t, carry):
            part[q, t, :, 0 : 2 * qw] = (
                dot_nn(xt[t, c], mine[:, 0 : 2 * qw]) + dot_nn(xts[t], theirs[:, 0 : 2 * qw])
            ).astype(BF16)
            part[q, t, :, 2 * qw : 3 * qw] = (
                dot_nn(ct[t, c], mine[:, 2 * qw :]) + dot_nn(cts[t], theirs[:, 2 * qw :])
            ).astype(BF16)
            return carry

        lax.fori_loop(0, n, one, 0)

    for k in range(1, stops):
        for copy in tok_copies(k):
            copy.start()
    ag_own(0)
    xa[0:rows, :] = tok_ref[...]
    ca[0:rows, :] = cot_ref[...]
    ma[0] = meta_ref[0]
    turn(0)
    for i in range(n - 1):
        ag_step(0, i)
    if nq > 1:
        ag_own(1)
    for k in range(1, stops):
        for copy in tok_copies(k):
            copy.wait_recv()
    for k in range(1, stops):
        turn(k)
    for copy in xt_copies():
        copy.start()
    gates = jnp.concatenate(
        [jnp.sum(pick_of(k) * ma[k, 1:2, :], axis=1, keepdims=True) for k in range(stops)]
    )
    gate_sum = jnp.zeros((stops * rows, 1), F32)
    for q in range(nq):
        if q >= 1:
            if q > 1:
                ag_step(q, 0)
            rs_step(q - 1, 0)
            for i in range(1, n - 1):
                ag_step(q, i)
                rs_step(q - 1, i)
            if q + 1 < nq:
                ag_own(q + 1)
        ag_join(q)
        gate_sum = gate_sum + forward(q, gates)
        if q == 0:
            if nq > 1:
                ag_step(1, 0)
            for copy in xt_copies():
                copy.wait_recv()
        terms(q)
    rs_step(nq - 1, 0)

    for k in range(stops):
        gt = gate_sum[k * rows : (k + 1) * rows]
        row = jnp.sum(pick_of(k) * gt, axis=0, keepdims=True)
        if k == 0:
            gate_ref[0] = jnp.broadcast_to(row, (8, span))
        else:
            gb[k] = jnp.broadcast_to(row, (8, span))
            gate_copy(k).start()
    for j in range(tiles):
        cut = slice(j * td, (j + 1) * td)
        out = sum(dot_nt(hid[q, c, :, 2 * qw :], w[q, cut, 2 * qw :]) for q in range(nq))
        tok = sum(dot_nt(hid[q, c, :, : 2 * qw], w[q, cut, : 2 * qw]) for q in range(nq))
        o0[:, cut] = out[:rows]
        t0[:, cut] = tok[:rows]
        for k in range(1, stops):
            ob[k, :, cut] = out[k * rows : (k + 1) * rows].astype(BF16)
            tb[k, :, cut] = tok[k * rows : (k + 1) * rows].astype(BF16)
            for copy in ret_copies(k, j):
                copy.start()
    for i in range(1, n - 1):
        rs_step(nq - 1, i)

    for k in range(1, stops):
        gate_copy(k).wait_recv()
        gate_ref[k] = rg[k]
        for j in range(tiles):
            for copy in ret_copies(k, j):
                copy.wait_recv()
    mixed, tgrad = o0[...], t0[...]
    for k in range(1, stops):
        mixed = mixed + ro[k].astype(F32)
        tgrad = tgrad + rt[k].astype(F32)
    mixed_ref[...] = mixed.astype(BF16)
    tgrad_ref[...] = tgrad.astype(BF16)
    for q in range(nq):
        rs_finish(q)

    for k in range(1, stops):
        for copy in tok_copies(k):
            copy.wait_send()
        gate_copy(k).wait_send()
        for j in range(tiles):
            for copy in ret_copies(k, j):
                copy.wait_send()
    for copy in xt_copies():
        copy.wait_send()
    for q in range(nq):
        hid_copy(q, c).wait_send()
        ag_sib(q, z, 0, c).wait_send()
        for i in range(n - 1):

            @pl.when((z - i >= 0) & has_r)
            def _():
                ag_right(q, i).wait_send()

            @pl.when((z + i <= n - 1) & has_l)
            def _():
                ag_left(q, i).wait_send()

            @pl.when(z - 1 - i >= 0)
            def _():
                ag_sib(q, z - 1 - i, 1 + i, c).wait_send()

            @pl.when(z + 1 + i <= n - 1)
            def _():
                ag_sib(q, z + 1 + i, n + i, c).wait_send()

            @pl.when(n - 1 - i > z)
            def _():
                rs_right(q, n - 1 - i).wait_send()

            @pl.when(i < z)
            def _():
                rs_left(q, i).wait_send()


def body(n_exp, n_dp, tokens, cotangent, w_in, w_out, block_rows, block_gates, block_count):
    stops = block_count.shape[1]
    block = block_rows.shape[2]
    span = block_rows.shape[1] // stops * block
    rows, width = tokens.shape
    sr, ffw = w_out.shape[1:]
    n, nq, total = n_dp // 2, ffw // LANES, stops * rows
    tiles = width // next(t for t in (512, 256, 128) if width % t == 0)
    entries = block_rows.reshape(stops, span)
    gates = block_gates.reshape(stops, span)
    positions = jnp.arange(span, dtype=jnp.int32)
    live = positions[None, :] // block < block_count[0][:, None]
    ids = jnp.where(live, entries, -1).astype(F32)
    pick = jnp.arange(8)[None, :, None]
    meta = jnp.where(pick == 0, ids[:, None, :], gates[:, None, :])

    dma = pltpu.SemaphoreType.DMA
    vmem = pltpu.VMEM
    mixed, tgrad, gate, gin, gout = pl.pallas_call(
        functools.partial(kernel, (n_exp, n_dp, stops)),
        out_shape=(
            jax.ShapeDtypeStruct((rows, width), BF16),
            jax.ShapeDtypeStruct((rows, width), BF16),
            jax.ShapeDtypeStruct((stops, 8, span), F32),
            jax.ShapeDtypeStruct((sr, 2 * ffw), BF16),
            jax.ShapeDtypeStruct((sr, ffw), BF16),
        ),
        in_specs=[pl.BlockSpec(memory_space=vmem)] * 5,
        out_specs=(pl.BlockSpec(memory_space=vmem),) * 5,
        scratch_shapes=[
            vmem((total, width), BF16),
            vmem((total, width), BF16),
            vmem((stops, 8, span), F32),
            vmem((nq, n_dp * sr, 3 * LANES), BF16),
            vmem((n, 2, sr, total), BF16),
            vmem((n, 2, sr, total), BF16),
            vmem((n, sr, total), BF16),
            vmem((n, sr, total), BF16),
            vmem((nq, 2, total, 3 * LANES), BF16),
            vmem((nq, n, sr, 3 * LANES), BF16),
            vmem((nq, n, sr, 3 * LANES), BF16),
            vmem((nq, n, sr, 3 * LANES), BF16),
            vmem((rows, width), F32),
            vmem((rows, width), F32),
            vmem((stops, rows, width), BF16),
            vmem((stops, rows, width), BF16),
            vmem((stops, 8, span), F32),
            vmem((stops, rows, width), BF16),
            vmem((stops, rows, width), BF16),
            vmem((stops, 8, span), F32),
            vmem((sr, 3 * LANES), F32),
            dma((nq, n)),
            dma((nq, n)),
            dma((nq, n)),
            dma((nq, n)),
            dma((nq, 2 * n)),
            dma((nq, 2 * n)),
            dma((2,)),
            dma((2,)),
            dma((nq,)),
            dma((nq,)),
            dma((nq, n)),
            dma((nq, n)),
            dma((nq, n)),
            dma((nq, n)),
            dma((stops, 3)),
            dma((stops, 3)),
            dma((stops, tiles, 2)),
            dma((stops, tiles, 2)),
            dma((stops,)),
            dma((stops,)),
        ],
        compiler_params=pltpu.CompilerParams(
            collective_id=0, has_side_effects=True, vmem_limit_bytes=56 * 1024 * 1024
        ),
        cost_estimate=pl.CostEstimate(
            flops=6 * total * width * 3 * ffw, bytes_accessed=8 * rows * width, transcendentals=0
        ),
    )(tokens, cotangent, w_in[0], w_out[0], meta)
    return mixed, tgrad, gate[:, 0].reshape(block_rows.shape), gin[None], gout[None]


def solution(mesh):
    in_specs = (
        P(("expert", "dp"), None),
        P(("expert", "dp"), None),
        P("expert", "dp", None),
        P("expert", "dp", None),
        P(("expert", "dp"), None, None),
        P(("expert", "dp"), None, None),
        P(("expert", "dp"), None),
    )
    out_specs = (
        P(("expert", "dp"), None),
        P(("expert", "dp"), None),
        P(("expert", "dp"), None, None),
        P("expert", "dp", None),
        P("expert", "dp", None),
    )
    run = functools.partial(body, mesh.shape["expert"], mesh.shape["dp"])
    return jax.shard_map(run, mesh=mesh, in_specs=in_specs, out_specs=out_specs, check_vma=False)
```

```python
import functools

import jax
import jax.numpy as jnp
from jax import lax
from jax.experimental import pallas as pl
from jax.experimental.pallas import tpu as pltpu
from jax.sharding import PartitionSpec as P

BF16, F32 = jnp.bfloat16, jnp.float32
MESH = pl.DeviceIdType.MESH
LANES = 128


def dot_nn(left, right):
    return jnp.dot(left, right, preferred_element_type=F32)


def dot_nt(left, right):
    return lax.dot_general(left, right, (((1,), (1,)), ((), ())), preferred_element_type=F32)


def kernel(
    dims,
    tok_ref,
    cot_ref,
    win_ref,
    wout_ref,
    meta_ref,
    mixed_ref,
    tgrad_ref,
    gate_ref,
    gin_ref,
    gout_ref,
    xa,
    ca,
    ma,
    w,
    xt,
    ct,
    xts,
    cts,
    hid,
    part,
    rbr,
    rbl,
    o0,
    t0,
    ob,
    tb,
    gb,
    ro,
    rt,
    rg,
    acc,
    s_ag,
    r_ag,
    s_sib,
    r_sib,
    s_xt,
    r_xt,
    s_hid,
    r_hid,
    s_rsr,
    r_rsr,
    s_rsl,
    r_rsl,
    s_tok,
    r_tok,
    s_ret,
    r_ret,
    s_rg,
    r_rg,
):
    n_exp, n_dp, stops = dims
    n = n_dp // 2
    rows, width = tok_ref.shape
    sr, ffw = wout_ref.shape
    qw = LANES
    nq = ffw // qw
    span = meta_ref.shape[2]
    td = next(t for t in (512, 256, 128) if width % t == 0)
    tiles = width // td

    e = lax.axis_index("expert")
    d = lax.axis_index("dp")
    z = d // 2
    c = d % 2
    has_l = z > 0
    has_r = z < n - 1
    right = {"expert": e, "dp": d + 2}
    left = {"expert": e, "dp": d - 2}
    sib = {"expert": e, "dp": 2 * z + (1 - c)}

    def cycle(k):
        return {"expert": (e + k) % n_exp, "dp": d}

    def lane_peer(i):
        return {"expert": e, "dp": 2 * ((z + i) % n) + c}

    def remote(src, dst, ss, rs, dev):
        return pltpu.make_async_remote_copy(
            src_ref=src, dst_ref=dst, send_sem=ss, recv_sem=rs, device_id=dev, device_id_type=MESH
        )

    offsets = sorted({k % n_exp for k in range(1, stops)} | {-k % n_exp for k in range(1, stops)})
    barrier = pltpu.get_barrier_semaphore()
    pl.semaphore_signal(barrier, inc=1, device_id=sib, device_id_type=MESH)
    for k in offsets:
        pl.semaphore_signal(barrier, inc=1, device_id=cycle(k), device_id_type=MESH)

    for i in range(1, n):
        pl.semaphore_signal(barrier, inc=1, device_id=lane_peer(i), device_id_type=MESH)

    own = pl.ds(pl.multiple_of(d * sr, 16), sr)
    for q in range(nq):
        w[q, own, 0:qw] = win_ref[:, q * qw : (q + 1) * qw]
        w[q, own, qw : 2 * qw] = win_ref[:, ffw + q * qw : ffw + (q + 1) * qw]
        w[q, own, 2 * qw : 3 * qw] = wout_ref[:, q * qw : (q + 1) * qw]
    pl.semaphore_wait(barrier, n + len(offsets))

    def shard(q, chip, core):
        return w.at[q, pl.ds(pl.multiple_of((2 * chip + core) * sr, 16), sr)]

    def ag_send(q, i):
        ref = shard(q, z, c)
        return remote(ref, ref, s_ag.at[q, i], r_ag.at[q, i], lane_peer(i))

    def ag_arrival(q, i):
        ref = shard(q, (z + n - i) % n, c)
        return remote(ref, ref, s_ag.at[q, i], r_ag.at[q, i], lane_peer(n - i))

    def ag_sib(q, i, core):
        ref = shard(q, (z + n - i) % n, core)
        return remote(ref, ref, s_sib.at[q, i], r_sib.at[q, i], sib)

    def tok_copies(k):
        cut = pl.ds(k * rows, rows)
        return [
            remote(tok_ref, xa.at[cut], s_tok.at[k, 0], r_tok.at[k, 0], cycle(-k)),
            remote(cot_ref, ca.at[cut], s_tok.at[k, 1], r_tok.at[k, 1], cycle(-k)),
            remote(meta_ref.at[k], ma.at[k], s_tok.at[k, 2], r_tok.at[k, 2], cycle(-k)),
        ]

    def xt_copies():
        return [
            remote(xt.at[:, 1 - c], xts, s_xt.at[0], r_xt.at[0], sib),
            remote(ct.at[:, 1 - c], cts, s_xt.at[1], r_xt.at[1], sib),
        ]

    def hid_copy(q, core):
        ref = hid.at[q, core]
        return remote(ref, ref, s_hid.at[q], r_hid.at[q], sib)

    def rs_right(q, t):
        return remote(part.at[q, t], rbr.at[q, t], s_rsr.at[q, t], r_rsr.at[q, t], right)

    def rs_left(q, t):
        return remote(part.at[q, t], rbl.at[q, t], s_rsl.at[q, t], r_rsl.at[q, t], left)

    def ret_copies(k, j):
        cut = (k, slice(None), pl.ds(j * td, td))
        return [
            remote(ob.at[cut], ro.at[cut], s_ret.at[k, j, 0], r_ret.at[k, j, 0], cycle(k)),
            remote(tb.at[cut], rt.at[cut], s_ret.at[k, j, 1], r_ret.at[k, j, 1], cycle(k)),
        ]

    def gate_copy(k):
        return remote(gb.at[k], rg.at[k], s_rg.at[k], r_rg.at[k], cycle(k))

    def ag_own(q):
        for i in range(1, n):
            ag_send(q, i).start()
        ag_sib(q, 0, c).start()

    def ag_join(q):
        for i in range(1, n):
            ag_arrival(q, i).wait_recv()
            ag_sib(q, i, c).start()
        for i in range(n):
            ag_sib(q, i, 1 - c).wait_recv()

    def rs_step(q, j):
        t = n - 1 - j

        @pl.when(t > z)
        def _():
            @pl.when(has_l)
            def _():
                rs_right(q, t).wait_recv()
                part[q, t] = (part[q, t].astype(F32) + rbr[q, t].astype(F32)).astype(BF16)

            rs_right(q, t).start()

        @pl.when(j < z)
        def _():
            @pl.when(has_r)
            def _():
                rs_left(q, j).wait_recv()
                part[q, j] = (part[q, j].astype(F32) + rbl[q, j].astype(F32)).astype(BF16)

            rs_left(q, j).start()

    def rs_finish(q):
        total = part[q, z].astype(F32)
        acc[...] = total

        @pl.when(has_l)
        def _():
            rs_right(q, z).wait_recv()
            acc[...] += rbr[q, z].astype(F32)

        @pl.when(has_r)
        def _():
            rs_left(q, z).wait_recv()
            acc[...] += rbl[q, z].astype(F32)

        done = acc[...].astype(BF16)
        gin_ref[:, q * qw : (q + 1) * qw] = done[:, 0:qw]
        gin_ref[:, ffw + q * qw : ffw + (q + 1) * qw] = done[:, qw : 2 * qw]
        gout_ref[:, q * qw : (q + 1) * qw] = done[:, 2 * qw : 3 * qw]

    def turn(k):
        cut = slice(k * rows, (k + 1) * rows)
        xt[:, :, :, cut] = xa[cut, :].T.reshape(n, 2, sr, rows)
        ct[:, :, :, cut] = ca[cut, :].T.reshape(n, 2, sr, rows)

    def pick_of(k):
        return jnp.where(
            lax.broadcasted_iota(jnp.int32, (rows, span), 0).astype(F32) == ma[k, 0:1, :], 1.0, 0.0
        )

    def forward(q, gates):
        pre = dot_nn(xa[...], w[q, :, 0 : 2 * qw])
        dc = dot_nn(ca[...], w[q, :, 2 * qw : 3 * qw])
        h, u = pre[:, :qw], pre[:, qw:]
        sig = jax.nn.sigmoid(h)
        act = h * sig
        a = act * u
        da = gates * dc
        hid[q, c, :, 0:qw] = (da * u * (sig * (1.0 + h * (1.0 - sig)))).astype(BF16)
        hid[q, c, :, qw : 2 * qw] = (da * act).astype(BF16)
        hid[q, c, :, 2 * qw : 3 * qw] = (gates * a).astype(BF16)
        hid_copy(q, c).start()
        return jnp.sum(a * dc, axis=1, keepdims=True)

    def terms(q):
        hid_copy(q, 1 - c).wait_recv()
        mine, theirs = hid[q, c], hid[q, 1 - c]

        def one(t, carry):
            part[q, t, :, 0 : 2 * qw] = (
                dot_nn(xt[t, c], mine[:, 0 : 2 * qw]) + dot_nn(xts[t], theirs[:, 0 : 2 * qw])
            ).astype(BF16)
            part[q, t, :, 2 * qw : 3 * qw] = (
                dot_nn(ct[t, c], mine[:, 2 * qw :]) + dot_nn(cts[t], theirs[:, 2 * qw :])
            ).astype(BF16)
            return carry

        lax.fori_loop(0, n, one, 0)

    for k in range(1, stops):
        for copy in tok_copies(k):
            copy.start()
    ag_own(0)
    xa[0:rows, :] = tok_ref[...]
    ca[0:rows, :] = cot_ref[...]
    ma[0] = meta_ref[0]
    turn(0)
    ag_join(0)
    if nq > 1:
        ag_own(1)
    for k in range(1, stops):
        for copy in tok_copies(k):
            copy.wait_recv()
    for k in range(1, stops):
        turn(k)
    for copy in xt_copies():
        copy.start()
    gates = jnp.concatenate(
        [jnp.sum(pick_of(k) * ma[k, 1:2, :], axis=1, keepdims=True) for k in range(stops)]
    )
    gate_sum = jnp.zeros((stops * rows, 1), F32)
    for q in range(nq):
        if q > 0:
            ag_join(q)
        gate_sum = gate_sum + forward(q, gates)
        if q == 0:
            for copy in xt_copies():
                copy.wait_recv()
        if q < nq - 1:
            terms(q)
            rs_step(q, 0)
            if q + 2 < nq:
                ag_own(q + 2)
            if q < nq - 2:
                for i in range(1, n - 1):
                    rs_step(q, i)

    for k in range(stops):
        gt = gate_sum[k * rows : (k + 1) * rows]
        row = jnp.sum(pick_of(k) * gt, axis=0, keepdims=True)
        if k == 0:
            gate_ref[0] = jnp.broadcast_to(row, (8, span))
        else:
            gb[k] = jnp.broadcast_to(row, (8, span))
            gate_copy(k).start()
    for j in range(tiles):
        cut = slice(j * td, (j + 1) * td)
        out = sum(dot_nt(hid[q, c, :, 2 * qw :], w[q, cut, 2 * qw :]) for q in range(nq))
        tok = sum(dot_nt(hid[q, c, :, : 2 * qw], w[q, cut, : 2 * qw]) for q in range(nq))
        o0[:, cut] = out[:rows]
        t0[:, cut] = tok[:rows]
        for k in range(1, stops):
            ob[k, :, cut] = out[k * rows : (k + 1) * rows].astype(BF16)
            tb[k, :, cut] = tok[k * rows : (k + 1) * rows].astype(BF16)
            for copy in ret_copies(k, j):
                copy.start()
    terms(nq - 1)
    for q in range(max(nq - 2, 0), nq):
        for i in range(0 if q == nq - 1 else 1, n - 1):
            rs_step(q, i)

    for k in range(1, stops):
        gate_copy(k).wait_recv()
        gate_ref[k] = rg[k]
        for j in range(tiles):
            for copy in ret_copies(k, j):
                copy.wait_recv()
    mixed, tgrad = o0[...], t0[...]
    for k in range(1, stops):
        mixed = mixed + ro[k].astype(F32)
        tgrad = tgrad + rt[k].astype(F32)
    mixed_ref[...] = mixed.astype(BF16)
    tgrad_ref[...] = tgrad.astype(BF16)
    for q in range(nq):
        rs_finish(q)

    for k in range(1, stops):
        for copy in tok_copies(k):
            copy.wait_send()
        gate_copy(k).wait_send()
        for j in range(tiles):
            for copy in ret_copies(k, j):
                copy.wait_send()
    for copy in xt_copies():
        copy.wait_send()
    for q in range(nq):
        hid_copy(q, c).wait_send()
        for i in range(n):
            ag_sib(q, i, c).wait_send()
        for i in range(1, n):
            ag_send(q, i).wait_send()
        for i in range(n - 1):

            @pl.when(n - 1 - i > z)
            def _():
                rs_right(q, n - 1 - i).wait_send()

            @pl.when(i < z)
            def _():
                rs_left(q, i).wait_send()


def body(n_exp, n_dp, tokens, cotangent, w_in, w_out, block_rows, block_gates, block_count):
    stops = block_count.shape[1]
    block = block_rows.shape[2]
    span = block_rows.shape[1] // stops * block
    rows, width = tokens.shape
    sr, ffw = w_out.shape[1:]
    n, nq, total = n_dp // 2, ffw // LANES, stops * rows
    tiles = width // next(t for t in (512, 256, 128) if width % t == 0)
    entries = block_rows.reshape(stops, span)
    gates = block_gates.reshape(stops, span)
    positions = jnp.arange(span, dtype=jnp.int32)
    live = positions[None, :] // block < block_count[0][:, None]
    ids = jnp.where(live, entries, -1).astype(F32)
    pick = jnp.arange(8)[None, :, None]
    meta = jnp.where(pick == 0, ids[:, None, :], gates[:, None, :])

    dma = pltpu.SemaphoreType.DMA
    vmem = pltpu.VMEM
    mixed, tgrad, gate, gin, gout = pl.pallas_call(
        functools.partial(kernel, (n_exp, n_dp, stops)),
        out_shape=(
            jax.ShapeDtypeStruct((rows, width), BF16),
            jax.ShapeDtypeStruct((rows, width), BF16),
            jax.ShapeDtypeStruct((stops, 8, span), F32),
            jax.ShapeDtypeStruct((sr, 2 * ffw), BF16),
            jax.ShapeDtypeStruct((sr, ffw), BF16),
        ),
        in_specs=[pl.BlockSpec(memory_space=vmem)] * 5,
        out_specs=(pl.BlockSpec(memory_space=vmem),) * 5,
        scratch_shapes=[
            vmem((total, width), BF16),
            vmem((total, width), BF16),
            vmem((stops, 8, span), F32),
            vmem((nq, n_dp * sr, 3 * LANES), BF16),
            vmem((n, 2, sr, total), BF16),
            vmem((n, 2, sr, total), BF16),
            vmem((n, sr, total), BF16),
            vmem((n, sr, total), BF16),
            vmem((nq, 2, total, 3 * LANES), BF16),
            vmem((nq, n, sr, 3 * LANES), BF16),
            vmem((nq, n, sr, 3 * LANES), BF16),
            vmem((nq, n, sr, 3 * LANES), BF16),
            vmem((rows, width), F32),
            vmem((rows, width), F32),
            vmem((stops, rows, width), BF16),
            vmem((stops, rows, width), BF16),
            vmem((stops, 8, span), F32),
            vmem((stops, rows, width), BF16),
            vmem((stops, rows, width), BF16),
            vmem((stops, 8, span), F32),
            vmem((sr, 3 * LANES), F32),
            dma((nq, n)),
            dma((nq, n)),
            dma((nq, n)),
            dma((nq, n)),
            dma((2,)),
            dma((2,)),
            dma((nq,)),
            dma((nq,)),
            dma((nq, n)),
            dma((nq, n)),
            dma((nq, n)),
            dma((nq, n)),
            dma((stops, 3)),
            dma((stops, 3)),
            dma((stops, tiles, 2)),
            dma((stops, tiles, 2)),
            dma((stops,)),
            dma((stops,)),
        ],
        compiler_params=pltpu.CompilerParams(
            collective_id=0, has_side_effects=True, vmem_limit_bytes=56 * 1024 * 1024
        ),
        cost_estimate=pl.CostEstimate(
            flops=6 * total * width * 3 * ffw, bytes_accessed=8 * rows * width, transcendentals=0
        ),
    )(tokens, cotangent, w_in[0], w_out[0], meta)
    return mixed, tgrad, gate[:, 0].reshape(block_rows.shape), gin[None], gout[None]


def solution(mesh):
    in_specs = (
        P(("expert", "dp"), None),
        P(("expert", "dp"), None),
        P("expert", "dp", None),
        P("expert", "dp", None),
        P(("expert", "dp"), None, None),
        P(("expert", "dp"), None, None),
        P(("expert", "dp"), None),
    )
    out_specs = (
        P(("expert", "dp"), None),
        P(("expert", "dp"), None),
        P(("expert", "dp"), None, None),
        P("expert", "dp", None),
        P("expert", "dp", None),
    )
    run = functools.partial(body, mesh.shape["expert"], mesh.shape["dp"])
    return jax.shard_map(run, mesh=mesh, in_specs=in_specs, out_specs=out_specs, check_vma=False)
```

```python
import functools

import jax
import jax.numpy as jnp
from jax import lax
from jax.experimental import pallas as pl
from jax.experimental.pallas import tpu as pltpu
from jax.sharding import PartitionSpec as P

BF16, F32 = jnp.bfloat16, jnp.float32
MESH = pl.DeviceIdType.MESH
LANES = 128


def dot_nn(left, right):
    return jnp.dot(left, right, preferred_element_type=F32)


def dot_nt(left, right):
    return lax.dot_general(left, right, (((1,), (1,)), ((), ())), preferred_element_type=F32)


def kernel(
    dims,
    tok_ref,
    cot_ref,
    win_ref,
    wout_ref,
    meta_ref,
    mixed_ref,
    tgrad_ref,
    gate_ref,
    gin_ref,
    gout_ref,
    xa,
    ca,
    ma,
    w,
    xt,
    ct,
    xts,
    cts,
    hid,
    part,
    rbr,
    rbl,
    o0,
    t0,
    ob,
    tb,
    gb,
    ro,
    rt,
    rg,
    acc,
    s_ag,
    r_ag,
    s_sib,
    r_sib,
    s_xt,
    r_xt,
    s_hid,
    r_hid,
    s_rsr,
    r_rsr,
    s_rsl,
    r_rsl,
    s_tok,
    r_tok,
    s_ret,
    r_ret,
    s_rg,
    r_rg,
):
    n_exp, n_dp, stops = dims
    n = n_dp // 2
    rows, width = tok_ref.shape
    sr, ffw = wout_ref.shape
    qw = LANES
    nq = ffw // qw
    span = meta_ref.shape[2]
    td = next(t for t in (512, 256, 128) if width % t == 0)
    tiles = width // td

    e = lax.axis_index("expert")
    d = lax.axis_index("dp")
    z = d // 2
    c = d % 2
    has_l = z > 0
    has_r = z < n - 1
    right = {"expert": e, "dp": d + 2}
    left = {"expert": e, "dp": d - 2}
    sib = {"expert": e, "dp": 2 * z + (1 - c)}

    def cycle(k):
        return {"expert": (e + k) % n_exp, "dp": d}

    def lane_peer(i):
        return {"expert": e, "dp": 2 * ((z + i) % n) + c}

    def remote(src, dst, ss, rs, dev):
        return pltpu.make_async_remote_copy(
            src_ref=src, dst_ref=dst, send_sem=ss, recv_sem=rs, device_id=dev, device_id_type=MESH
        )

    offsets = sorted({k % n_exp for k in range(1, stops)} | {-k % n_exp for k in range(1, stops)})
    barrier = pltpu.get_barrier_semaphore()
    pl.semaphore_signal(barrier, inc=1, device_id=sib, device_id_type=MESH)
    for k in offsets:
        pl.semaphore_signal(barrier, inc=1, device_id=cycle(k), device_id_type=MESH)

    for i in range(1, n):
        pl.semaphore_signal(barrier, inc=1, device_id=lane_peer(i), device_id_type=MESH)

    own = pl.ds(pl.multiple_of(d * sr, 16), sr)
    for q in range(nq):
        w[q, own, 0:qw] = win_ref[:, q * qw : (q + 1) * qw]
        w[q, own, qw : 2 * qw] = win_ref[:, ffw + q * qw : ffw + (q + 1) * qw]
        w[q, own, 2 * qw : 3 * qw] = wout_ref[:, q * qw : (q + 1) * qw]
    pl.semaphore_wait(barrier, n + len(offsets))

    def shard(q, chip, core):
        return w.at[q, pl.ds(pl.multiple_of((2 * chip + core) * sr, 16), sr)]

    def ag_send(q, i):
        ref = shard(q, z, c)
        return remote(ref, ref, s_ag.at[q, i], r_ag.at[q, i], lane_peer(i))

    def ag_arrival(q, i):
        ref = shard(q, (z + n - i) % n, c)
        return remote(ref, ref, s_ag.at[q, i], r_ag.at[q, i], lane_peer(n - i))

    def ag_sib(q, i, core):
        ref = shard(q, (z + n - i) % n, core)
        return remote(ref, ref, s_sib.at[q, i], r_sib.at[q, i], sib)

    def tok_copies(k):
        cut = pl.ds(k * rows, rows)
        return [
            remote(tok_ref, xa.at[cut], s_tok.at[k, 0], r_tok.at[k, 0], cycle(-k)),
            remote(cot_ref, ca.at[cut], s_tok.at[k, 1], r_tok.at[k, 1], cycle(-k)),
            remote(meta_ref.at[k], ma.at[k], s_tok.at[k, 2], r_tok.at[k, 2], cycle(-k)),
        ]

    def xt_copies():
        return [
            remote(xt.at[:, 1 - c], xts, s_xt.at[0], r_xt.at[0], sib),
            remote(ct.at[:, 1 - c], cts, s_xt.at[1], r_xt.at[1], sib),
        ]

    def hid_copy(q, core):
        ref = hid.at[q, core]
        return remote(ref, ref, s_hid.at[q], r_hid.at[q], sib)

    def rs_right(q, t):
        return remote(part.at[q, t], rbr.at[q, t], s_rsr.at[q, t], r_rsr.at[q, t], right)

    def rs_left(q, t):
        return remote(part.at[q, t], rbl.at[q, t], s_rsl.at[q, t], r_rsl.at[q, t], left)

    def ret_copies(k, j):
        cut = (k, slice(None), pl.ds(j * td, td))
        return [
            remote(ob.at[cut], ro.at[cut], s_ret.at[k, j, 0], r_ret.at[k, j, 0], cycle(k)),
            remote(tb.at[cut], rt.at[cut], s_ret.at[k, j, 1], r_ret.at[k, j, 1], cycle(k)),
        ]

    def gate_copy(k):
        return remote(gb.at[k], rg.at[k], s_rg.at[k], r_rg.at[k], cycle(k))

    def ag_own(q):
        for i in range(1, n):
            ag_send(q, i).start()
        ag_sib(q, 0, c).start()

    def ag_join(q):
        for i in range(1, n):
            ag_arrival(q, i).wait_recv()
            ag_sib(q, i, c).start()
        for i in range(n):
            ag_sib(q, i, 1 - c).wait_recv()

    def rs_step(q, i):
        @pl.when(i >= z)
        def _():
            t = n - 1 - i + z

            @pl.when(has_l)
            def _():
                rs_right(q, t).wait_recv()
                part[q, t] = (part[q, t].astype(F32) + rbr[q, t].astype(F32)).astype(BF16)

            rs_right(q, t).start()

        @pl.when(i >= n - 1 - z)
        def _():
            t = i - (n - 1 - z)

            @pl.when(has_r)
            def _():
                rs_left(q, t).wait_recv()
                part[q, t] = (part[q, t].astype(F32) + rbl[q, t].astype(F32)).astype(BF16)

            rs_left(q, t).start()

    def rs_finish(q):
        total = part[q, z].astype(F32)
        acc[...] = total

        @pl.when(has_l)
        def _():
            rs_right(q, z).wait_recv()
            acc[...] += rbr[q, z].astype(F32)

        @pl.when(has_r)
        def _():
            rs_left(q, z).wait_recv()
            acc[...] += rbl[q, z].astype(F32)

        done = acc[...].astype(BF16)
        gin_ref[:, q * qw : (q + 1) * qw] = done[:, 0:qw]
        gin_ref[:, ffw + q * qw : ffw + (q + 1) * qw] = done[:, qw : 2 * qw]
        gout_ref[:, q * qw : (q + 1) * qw] = done[:, 2 * qw : 3 * qw]

    def turn(k):
        cut = slice(k * rows, (k + 1) * rows)
        xt[:, :, :, cut] = xa[cut, :].T.reshape(n, 2, sr, rows)
        ct[:, :, :, cut] = ca[cut, :].T.reshape(n, 2, sr, rows)

    def pick_of(k):
        return jnp.where(
            lax.broadcasted_iota(jnp.int32, (rows, span), 0).astype(F32) == ma[k, 0:1, :], 1.0, 0.0
        )

    def forward(q, gates):
        pre = dot_nn(xa[...], w[q, :, 0 : 2 * qw])
        dc = dot_nn(ca[...], w[q, :, 2 * qw : 3 * qw])
        h, u = pre[:, :qw], pre[:, qw:]
        sig = jax.nn.sigmoid(h)
        act = h * sig
        a = act * u
        da = gates * dc
        hid[q, c, :, 0:qw] = (da * u * (sig * (1.0 + h * (1.0 - sig)))).astype(BF16)
        hid[q, c, :, qw : 2 * qw] = (da * act).astype(BF16)
        hid[q, c, :, 2 * qw : 3 * qw] = (gates * a).astype(BF16)
        hid_copy(q, c).start()
        return jnp.sum(a * dc, axis=1, keepdims=True)

    def terms(q):
        hid_copy(q, 1 - c).wait_recv()
        mine, theirs = hid[q, c], hid[q, 1 - c]

        def one(t, carry):
            part[q, t, :, 0 : 2 * qw] = (
                dot_nn(xt[t, c], mine[:, 0 : 2 * qw]) + dot_nn(xts[t], theirs[:, 0 : 2 * qw])
            ).astype(BF16)
            part[q, t, :, 2 * qw : 3 * qw] = (
                dot_nn(ct[t, c], mine[:, 2 * qw :]) + dot_nn(cts[t], theirs[:, 2 * qw :])
            ).astype(BF16)
            return carry

        lax.fori_loop(0, n, one, 0)

    for k in range(1, stops):
        for copy in tok_copies(k):
            copy.start()
    ag_own(0)
    xa[0:rows, :] = tok_ref[...]
    ca[0:rows, :] = cot_ref[...]
    ma[0] = meta_ref[0]
    turn(0)
    ag_join(0)
    if nq > 1:
        ag_own(1)
    for k in range(1, stops):
        for copy in tok_copies(k):
            copy.wait_recv()
    for k in range(1, stops):
        turn(k)
    for copy in xt_copies():
        copy.start()
    gates = jnp.concatenate(
        [jnp.sum(pick_of(k) * ma[k, 1:2, :], axis=1, keepdims=True) for k in range(stops)]
    )
    gate_sum = jnp.zeros((stops * rows, 1), F32)
    for q in range(nq):
        if q > 0:
            ag_join(q)
        gate_sum = gate_sum + forward(q, gates)
        if q == 0:
            for copy in xt_copies():
                copy.wait_recv()
        if q < nq - 1:
            terms(q)
            rs_step(q, 0)
            if q + 2 < nq:
                ag_own(q + 2)
            if q < nq - 2:
                for i in range(1, n - 1):
                    rs_step(q, i)

    for k in range(stops):
        gt = gate_sum[k * rows : (k + 1) * rows]
        row = jnp.sum(pick_of(k) * gt, axis=0, keepdims=True)
        if k == 0:
            gate_ref[0] = jnp.broadcast_to(row, (8, span))
        else:
            gb[k] = jnp.broadcast_to(row, (8, span))
            gate_copy(k).start()
    for j in range(tiles):
        cut = slice(j * td, (j + 1) * td)
        out = sum(dot_nt(hid[q, c, :, 2 * qw :], w[q, cut, 2 * qw :]) for q in range(nq))
        tok = sum(dot_nt(hid[q, c, :, : 2 * qw], w[q, cut, : 2 * qw]) for q in range(nq))
        o0[:, cut] = out[:rows]
        t0[:, cut] = tok[:rows]
        for k in range(1, stops):
            ob[k, :, cut] = out[k * rows : (k + 1) * rows].astype(BF16)
            tb[k, :, cut] = tok[k * rows : (k + 1) * rows].astype(BF16)
            for copy in ret_copies(k, j):
                copy.start()
    terms(nq - 1)
    rs_step(nq - 1, 0)
    for i in range(1, n - 1):
        if nq > 1:
            rs_step(nq - 2, i)
        rs_step(nq - 1, i)

    for k in range(1, stops):
        gate_copy(k).wait_recv()
        gate_ref[k] = rg[k]
        for j in range(tiles):
            for copy in ret_copies(k, j):
                copy.wait_recv()
    mixed, tgrad = o0[...], t0[...]
    for k in range(1, stops):
        mixed = mixed + ro[k].astype(F32)
        tgrad = tgrad + rt[k].astype(F32)
    mixed_ref[...] = mixed.astype(BF16)
    tgrad_ref[...] = tgrad.astype(BF16)
    for q in range(nq):
        rs_finish(q)

    for k in range(1, stops):
        for copy in tok_copies(k):
            copy.wait_send()
        gate_copy(k).wait_send()
        for j in range(tiles):
            for copy in ret_copies(k, j):
                copy.wait_send()
    for copy in xt_copies():
        copy.wait_send()
    for q in range(nq):
        hid_copy(q, c).wait_send()
        for i in range(n):
            ag_sib(q, i, c).wait_send()
        for i in range(1, n):
            ag_send(q, i).wait_send()
        for i in range(n - 1):

            @pl.when(n - 1 - i > z)
            def _():
                rs_right(q, n - 1 - i).wait_send()

            @pl.when(i < z)
            def _():
                rs_left(q, i).wait_send()


def body(n_exp, n_dp, tokens, cotangent, w_in, w_out, block_rows, block_gates, block_count):
    stops = block_count.shape[1]
    block = block_rows.shape[2]
    span = block_rows.shape[1] // stops * block
    rows, width = tokens.shape
    sr, ffw = w_out.shape[1:]
    n, nq, total = n_dp // 2, ffw // LANES, stops * rows
    tiles = width // next(t for t in (512, 256, 128) if width % t == 0)
    entries = block_rows.reshape(stops, span)
    gates = block_gates.reshape(stops, span)
    positions = jnp.arange(span, dtype=jnp.int32)
    live = positions[None, :] // block < block_count[0][:, None]
    ids = jnp.where(live, entries, -1).astype(F32)
    pick = jnp.arange(8)[None, :, None]
    meta = jnp.where(pick == 0, ids[:, None, :], gates[:, None, :])

    dma = pltpu.SemaphoreType.DMA
    vmem = pltpu.VMEM
    mixed, tgrad, gate, gin, gout = pl.pallas_call(
        functools.partial(kernel, (n_exp, n_dp, stops)),
        out_shape=(
            jax.ShapeDtypeStruct((rows, width), BF16),
            jax.ShapeDtypeStruct((rows, width), BF16),
            jax.ShapeDtypeStruct((stops, 8, span), F32),
            jax.ShapeDtypeStruct((sr, 2 * ffw), BF16),
            jax.ShapeDtypeStruct((sr, ffw), BF16),
        ),
        in_specs=[pl.BlockSpec(memory_space=vmem)] * 5,
        out_specs=(pl.BlockSpec(memory_space=vmem),) * 5,
        scratch_shapes=[
            vmem((total, width), BF16),
            vmem((total, width), BF16),
            vmem((stops, 8, span), F32),
            vmem((nq, n_dp * sr, 3 * LANES), BF16),
            vmem((n, 2, sr, total), BF16),
            vmem((n, 2, sr, total), BF16),
            vmem((n, sr, total), BF16),
            vmem((n, sr, total), BF16),
            vmem((nq, 2, total, 3 * LANES), BF16),
            vmem((nq, n, sr, 3 * LANES), BF16),
            vmem((nq, n, sr, 3 * LANES), BF16),
            vmem((nq, n, sr, 3 * LANES), BF16),
            vmem((rows, width), F32),
            vmem((rows, width), F32),
            vmem((stops, rows, width), BF16),
            vmem((stops, rows, width), BF16),
            vmem((stops, 8, span), F32),
            vmem((stops, rows, width), BF16),
            vmem((stops, rows, width), BF16),
            vmem((stops, 8, span), F32),
            vmem((sr, 3 * LANES), F32),
            dma((nq, n)),
            dma((nq, n)),
            dma((nq, n)),
            dma((nq, n)),
            dma((2,)),
            dma((2,)),
            dma((nq,)),
            dma((nq,)),
            dma((nq, n)),
            dma((nq, n)),
            dma((nq, n)),
            dma((nq, n)),
            dma((stops, 3)),
            dma((stops, 3)),
            dma((stops, tiles, 2)),
            dma((stops, tiles, 2)),
            dma((stops,)),
            dma((stops,)),
        ],
        compiler_params=pltpu.CompilerParams(
            collective_id=0, has_side_effects=True, vmem_limit_bytes=56 * 1024 * 1024
        ),
        cost_estimate=pl.CostEstimate(
            flops=6 * total * width * 3 * ffw, bytes_accessed=8 * rows * width, transcendentals=0
        ),
    )(tokens, cotangent, w_in[0], w_out[0], meta)
    return mixed, tgrad, gate[:, 0].reshape(block_rows.shape), gin[None], gout[None]


def solution(mesh):
    in_specs = (
        P(("expert", "dp"), None),
        P(("expert", "dp"), None),
        P("expert", "dp", None),
        P("expert", "dp", None),
        P(("expert", "dp"), None, None),
        P(("expert", "dp"), None, None),
        P(("expert", "dp"), None),
    )
    out_specs = (
        P(("expert", "dp"), None),
        P(("expert", "dp"), None),
        P(("expert", "dp"), None, None),
        P("expert", "dp", None),
        P("expert", "dp", None),
    )
    run = functools.partial(body, mesh.shape["expert"], mesh.shape["dp"])
    return jax.shard_map(run, mesh=mesh, in_specs=in_specs, out_specs=out_specs, check_vma=False)
```
